32 devices in a mesh: row: 8 (over y, x, core), col: 4 (over z).
Axes of the slice: x: 2, y: 2, z: 4, core: 2. Of those that a mesh axis runs over, the one named last changes fastest.
Arguments:
- covariance: float32 [2048, 2048], P('row', 'col'), may hold values from 0 to 4, as said below
- panels: int32 [4], replicated, may hold values from 0 to 7, as said below
- observed: float32 [2048], P('row'), may hold values from -6 to 6
- drift_basis: float32 [64, 2048], P(None, 'row'), may hold values from -1.5 to 1.5
Outputs:
- complement: float32 [2048, 2048], P('row', 'col')
- factor: float32 [2048, 1024], P('row')
- solved_data: float32 [2048], P('row')
- solved_drift: float32 [64, 2048], P(None, 'row')
The draws below stay inside these ranges and needn't reach their ends.
Inputs may be any that keep to these rules, and one draw needn't show every extreme that they name: `covariance`: symmetric and positive definite. `panels`: 4 different tile indices; tile 8 - 1 is always among them.
All inputs are finite; a program needn't handle non-finite values.
Results may differ from the reference program's by a relative error of at most 0.0003.
Values sent between devices are 32-bit elements; how exact they have to be, the bound alone decides.
A program may use at most 64 MiB of HBM per device.

```python
import math
import jax
import jax.numpy as jnp
from jax import lax

B = 256
DR = 64
K = 4
NT = 8
NS = 2048


def site_points(key):
    lattice = jax.random.randint(jax.random.fold_in(key, 11), (NS, 2), 0, 4096)
    return lattice.astype(jnp.float32) * (1.0 / 4096.0)


def draw_covariance(key, part):
    points = site_points(key)
    corr_range = 0.05
    nugget = jnp.exp(jax.random.uniform(jax.random.fold_in(key, 12), (NS,), jnp.float32, math.log(0.3), math.log(1.5)))
    delta_x = points[:, 0][:, None] - points[:, 0][None, :]
    delta_y = points[:, 1][:, None] - points[:, 1][None, :]
    scaled = jnp.sqrt(delta_x * delta_x + delta_y * delta_y) * (math.sqrt(3.0) / corr_range)
    matern = (1.0 + scaled) * jnp.exp(-scaled)
    return (matern + jnp.diag(nugget)).astype(jnp.float32)


def draw_drift_basis(key, part):
    points = site_points(key)
    freqs = jax.random.normal(jax.random.fold_in(key, 21), (DR, 2), jnp.float32) * 4.0
    phases = jax.random.uniform(jax.random.fold_in(key, 22), (DR, 1), jnp.float32, 0.0, 2.0 * math.pi)
    angles = 2.0 * math.pi * (freqs[:, 0:1] * points[:, 0][None, :] + freqs[:, 1:2] * points[:, 1][None, :]) + phases
    return (math.sqrt(2.0) * jnp.cos(angles)).astype(jnp.float32)


def draw_panels(key, part):
    others = jax.random.permutation(jax.random.fold_in(key, 31), NT - 1)[:K - 1]
    chosen = jnp.concatenate([others.astype(jnp.int32), jnp.full((1,), NT - 1, jnp.int32)])
    shuffle = jax.random.permutation(jax.random.fold_in(key, 32), K)
    return chosen[shuffle].astype(jnp.int32)


def level_of(key, shape, pieces, smallest, largest):
    def one(dim, shards_of):
        heights = jax.random.uniform(jax.random.fold_in(jax.random.fold_in(key, 6), dim), (shards_of,), jnp.float32, smallest / len(pieces), largest / len(pieces))
        return jnp.repeat(jnp.exp(heights), shape[dim] // shards_of).reshape((-1,) + (1,) * (len(shape) - dim - 1))

    level = one(*pieces[0])
    for cut in pieces[1:]:
        level = level * one(*cut)
    return level


def noise(key, extent, scale, limit, cuts=(), held_as=jnp.bfloat16):
    factor_of = level_of(key, extent, cuts, -0.22, 0.18) if cuts else 1.0
    array = jax.random.normal(key, extent, jnp.float32) * scale * factor_of
    return jnp.minimum(jnp.maximum(array, -limit), limit).astype(held_as)


def setup_inputs(seed: int = 0) -> dict:
    keys = jax.random.split(jax.random.key(seed), 5)
    covariance = draw_covariance(jax.random.fold_in(keys[4], 71), 0)
    panels = draw_panels(jax.random.fold_in(keys[4], 71), 0)
    observed = noise(keys[2], (NS,), 1.0, 6.0, ((0, 8),), jnp.float32)
    drift_basis = draw_drift_basis(jax.random.fold_in(keys[4], 71), 0)
    return {"covariance": covariance, "panels": panels, "observed": observed, "drift_basis": drift_basis}


def solve_right(chol_tile, values):
    return lax.linalg.triangular_solve(chol_tile, values, left_side=False, lower=True, transpose_a=True)

def reference(covariance, panels, observed, drift_basis):
    sites = covariance.shape[0]
    tile_ids = lax.iota(jnp.int32, sites) // B
    matrix = covariance
    sides = jnp.concatenate([observed[None, :], drift_basis], axis=0)
    factors = []
    for position in range(K):
        target = panels[position]
        offset = (target * B).astype(jnp.int32)
        keep = jnp.all(tile_ids[:, None] != panels[:position][None, :], axis=1).astype(matrix.dtype)
        column = lax.dynamic_slice_in_dim(matrix, offset, B, 1)
        diag_tile = lax.dynamic_slice_in_dim(column, offset, B, 0)
        chol_tile = jnp.linalg.cholesky(diag_tile)
        panel = solve_right(chol_tile, column) * keep[:, None]
        matrix = matrix - lax.dot_general(panel, panel, (((1,), (1,)), ((), ())), precision=lax.Precision.HIGHEST)
        side_tile = lax.dynamic_slice_in_dim(sides, offset, B, 1)
        solved = solve_right(chol_tile, side_tile)
        sides = sides - lax.dot_general(solved, panel, (((1,), (1,)), ((), ())), precision=lax.Precision.HIGHEST)
        placed = lax.dynamic_update_slice_in_dim(jnp.zeros_like(sides), solved, offset, 1)
        sides = jnp.where((tile_ids == target)[None, :], placed, sides)
        factors.append(panel)
    keep_all = jnp.all(tile_ids[:, None] != panels[None, :], axis=1).astype(matrix.dtype)
    complement = matrix * keep_all[:, None] * keep_all[None, :]
    return (complement, jnp.concatenate(factors, axis=1), sides[0], sides[1:])
```

```python
import functools

import jax
import jax.numpy as jnp
from jax import lax
from jax.experimental import pallas as pl
from jax.experimental.pallas import tpu as pltpu
from jax.sharding import PartitionSpec as P

B = 256
K = 4
STRIP = 32
GROUP = 8
LANES = 128
SIDES = 72


def split(value):
    high = value.astype(jnp.bfloat16)
    low = (value - high.astype(jnp.float32)).astype(jnp.bfloat16)
    return high, low


def product(left, right, dims=((1,), (0,))):
    one = functools.partial(
        lax.dot_general,
        dimension_numbers=(dims, ((), ())),
        preferred_element_type=jnp.float32,
    )
    return one(left[0], right[0]) + (one(left[0], right[1]) + one(left[1], right[0]))


def eliminate_strip(strip, base):
    halves = [strip[:, h * LANES : (h + 1) * LANES] for h in range(B // LANES)]
    done = [[] for _ in halves]
    lane = lax.broadcasted_iota(jnp.int32, (1, LANES), 1)
    for group in range(STRIP // GROUP):
        rows = STRIP - group * GROUP
        row = lax.broadcasted_iota(jnp.int32, (rows, 1), 0)
        first = base + group * GROUP
        home, where = first // LANES, first % LANES
        columns = [
            jnp.broadcast_to(halves[home][:, where + c : where + c + 1], (rows, LANES))
            for c in range(GROUP)
        ]
        for c in range(GROUP):
            scale = lax.rsqrt(columns[c][c : c + 1, :])
            below = row > c
            factor = jnp.where(below, columns[c] * scale, 0.0)
            for d in range(c + 1, GROUP):
                columns[d] = columns[d] - factor * (columns[d][c : c + 1, :] * scale)
            for h in range(len(halves)):
                pivot = halves[h][c : c + 1, :] * scale
                rest = halves[h]
                if h == home:
                    here = lane == where + c
                    pivot = jnp.where(here, scale, pivot)
                    rest = jnp.where(here & below, 0.0, rest)
                halves[h] = jnp.where(row == c, pivot, rest - factor * pivot)
        for h in range(len(halves)):
            done[h].append(halves[h][:GROUP])
            halves[h] = halves[h][GROUP:]
    return jnp.concatenate([jnp.concatenate(part, axis=0) for part in done], axis=1)


def invert_factor(tile_ref):
    lane = lax.broadcasted_iota(jnp.int32, (1, B), 1)
    for base in range(0, B, STRIP):
        strip = eliminate_strip(tile_ref[base : base + STRIP, :], base)
        tile_ref[base : base + STRIP, :] = strip
        after = base + STRIP
        if after < B:
            own = (lane >= base) & (lane < after)
            pivot = base + lax.broadcasted_iota(jnp.int32, (STRIP, 1), 0)
            halves = split(jnp.where(own & (lane > pivot), 0.0, strip))
            turned = split(strip[:, after:].T)
            trailing = jnp.where(own, 0.0, tile_ref[after:, :])
            tile_ref[after:, :] = trailing - product(turned, halves)
    row = lax.broadcasted_iota(jnp.int32, (B, B), 0)
    col = lax.broadcasted_iota(jnp.int32, (B, B), 1)
    return jnp.where(row >= col, tile_ref[...], 0.0)


def tile_at(index):
    return pl.ds(pl.multiple_of(index * B, B), B)


def compute_kernel(
    panels, place, among, sides_among, block, sides, complement, factor, solved, work, sides_work, tile
):
    cols_here = block.shape[1]
    col_tiles = cols_here // B
    row_tile = place[0]
    first_col = place[1]
    work[...] = among[...]
    sides_work[...] = sides_among[...]
    complement[...] = block[...]
    solved[...] = sides[...]

    def step(p, gone):
        target = panels[p]
        tile[...] = work[tile_at(p), tile_at(p)]
        inverse = split(invert_factor(tile))

        def scale_tile(c, _):
            work[tile_at(p), tile_at(c)] = product(inverse, split(work[tile_at(p), tile_at(c)]))
            return 0

        lax.fori_loop(p, K + col_tiles + 1, scale_tile, 0)
        side = product(split(sides_work[:, tile_at(p)]), inverse, ((1,), (1,)))
        side_halves = split(side)

        def update_row(q, _):
            across = work[tile_at(p), tile_at(q)]
            turned = split(across.T)

            def update_tile(c, _):
                work[tile_at(q), tile_at(c)] -= product(turned, split(work[tile_at(p), tile_at(c)]))
                return 0

            lax.fori_loop(q, K + col_tiles + 1, update_tile, 0)
            sides_work[:, tile_at(q)] -= product(side_halves, split(across))
            return 0

        lax.fori_loop(p + 1, K, update_row, 0)
        mine = work[tile_at(p), pl.ds(K * B + cols_here, B)]
        mine = mine * (1.0 - gone)
        turned = mine.T
        factor[:, tile_at(p)] = turned
        turned = split(turned)
        for c in range(col_tiles):
            part = work[tile_at(p), pl.ds((K + c) * B, B)]
            complement[:, c * B : (c + 1) * B] -= product(turned, split(part))
        rest = solved[...] - product(side_halves, split(mine))
        solved[...] = jnp.where(row_tile == target, side, rest)
        return jnp.where(row_tile == target, 1.0, gone)

    gone = lax.fori_loop(0, K, step, jnp.float32(0.0))
    for c in range(col_tiles):
        keep = 1.0 - gone
        for p in range(K):
            keep = jnp.where(panels[p] == first_col + c, 0.0, keep)
        complement[:, c * B : (c + 1) * B] *= keep


def compute(panels, place, among, sides_among, block, sides):
    rows_here, cols_here = block.shape
    vmem = pl.BlockSpec(memory_space=pltpu.VMEM)
    smem = pl.BlockSpec(memory_space=pltpu.SMEM)
    return pl.pallas_call(
        compute_kernel,
        out_shape=(
            jax.ShapeDtypeStruct((rows_here, cols_here), jnp.float32),
            jax.ShapeDtypeStruct((rows_here, K * B), jnp.float32),
            jax.ShapeDtypeStruct(sides.shape, jnp.float32),
        ),
        in_specs=[smem, smem, vmem, vmem, vmem, vmem],
        out_specs=(vmem, vmem, vmem),
        scratch_shapes=[
            pltpu.VMEM(among.shape, jnp.float32),
            pltpu.VMEM(sides_among.shape, jnp.float32),
            pltpu.VMEM((B, B), jnp.float32),
        ],
        compiler_params=pltpu.CompilerParams(vmem_limit_bytes=56 * 1024 * 1024),
        cost_estimate=pl.CostEstimate(flops=10**10, bytes_accessed=10**7, transcendentals=0),
    )(panels, place, among, sides_among, block, sides)


def gather_panels(panels, row_tile, first_col, block, sides):
    cols_here = block.shape[1]
    col_tiles = cols_here // B
    mine = (panels == row_tile).astype(jnp.float32)
    rows = lax.psum((mine[:, None, None] * block[None]).reshape(K * B, cols_here), "row")
    sides_among = lax.psum(mine[:, None, None] * sides[None], "row")
    sides_among = sides_among.transpose(1, 0, 2).reshape(SIDES, K * B)
    parts = []
    for wanted in [panels[p] for p in range(K)] + [row_tile]:
        local = wanted - first_col
        held = (local >= 0) & (local < col_tiles)
        part = lax.dynamic_slice_in_dim(rows, jnp.clip(local, 0, col_tiles - 1) * B, B, 1)
        parts.append(jnp.where(held, part, 0.0))
    spread = lax.psum(jnp.concatenate(parts, axis=1), "col")
    return jnp.concatenate([spread[:, : K * B], rows, spread[:, K * B :]], axis=1), sides_among


def on_device(covariance, panels, observed, drift_basis):
    rows_here, cols_here = covariance.shape
    row_tile = lax.axis_index("row")
    first_col = lax.axis_index("col") * (cols_here // B)
    drifts = drift_basis.shape[0]
    sides = jnp.concatenate(
        [observed[None, :], drift_basis, jnp.zeros((SIDES - 1 - drifts, rows_here), jnp.float32)], axis=0
    )
    among, sides_among = gather_panels(panels, row_tile, first_col, covariance, sides)
    place = jnp.stack([row_tile, first_col]).astype(jnp.int32)
    complement, factor, solved = compute(panels, place, among, sides_among, covariance, sides)
    return complement, factor, solved[0], solved[1 : 1 + drifts]


def solution(mesh):
    return jax.shard_map(
        on_device,
        mesh=mesh,
        in_specs=(P("row", "col"), P(), P("row"), P(None, "row")),
        out_specs=(P("row", "col"), P("row", None), P("row"), P(None, "row")),
        check_vma=False,
    )
```

```python
import functools

import jax
import jax.numpy as jnp
from jax import lax
from jax.experimental import pallas as pl
from jax.experimental.pallas import tpu as pltpu
from jax.sharding import PartitionSpec as P

B = 256
K = 4
STRIP = 32
GROUP = 8
LANES = 128
SIDES = 128
SHARES = 8
SHARE = B // SHARES


def split(value):
    high = value.astype(jnp.bfloat16)
    low = (value - high.astype(jnp.float32)).astype(jnp.bfloat16)
    return high, low


def product(left, right, dims=((1,), (0,))):
    one = functools.partial(
        lax.dot_general,
        dimension_numbers=(dims, ((), ())),
        preferred_element_type=jnp.float32,
    )
    return one(left[0], right[0]) + (one(left[0], right[1]) + one(left[1], right[0]))


def eliminate_strip(strip, base):
    halves = [strip[:, h * LANES : (h + 1) * LANES] for h in range(B // LANES)]
    done = [[] for _ in halves]
    lane = lax.broadcasted_iota(jnp.int32, (1, LANES), 1)
    for group in range(STRIP // GROUP):
        rows = STRIP - group * GROUP
        row = lax.broadcasted_iota(jnp.int32, (rows, 1), 0)
        first = base + group * GROUP
        home, where = first // LANES, first % LANES
        columns = [
            jnp.broadcast_to(halves[home][:, where + c : where + c + 1], (rows, LANES))
            for c in range(GROUP)
        ]
        for c in range(GROUP):
            scale = lax.rsqrt(columns[c][c : c + 1, :])
            below = row > c
            factor = jnp.where(below, columns[c] * scale, 0.0)
            for d in range(c + 1, GROUP):
                columns[d] = columns[d] - factor * (columns[d][c : c + 1, :] * scale)
            for h in range(len(halves)):
                pivot = halves[h][c : c + 1, :] * scale
                rest = halves[h]
                if h == home:
                    here = lane == where + c
                    pivot = jnp.where(here, scale, pivot)
                    rest = jnp.where(here & below, 0.0, rest)
                halves[h] = jnp.where(row == c, pivot, rest - factor * pivot)
        for h in range(len(halves)):
            done[h].append(halves[h][:GROUP])
            halves[h] = halves[h][GROUP:]
    return jnp.concatenate([jnp.concatenate(part, axis=0) for part in done], axis=1)


def invert_factor(tile_ref):
    lane = lax.broadcasted_iota(jnp.int32, (1, B), 1)
    for base in range(0, B, STRIP):
        strip = eliminate_strip(tile_ref[base : base + STRIP, :], base)
        tile_ref[base : base + STRIP, :] = strip
        after = base + STRIP
        if after < B:
            own = (lane >= base) & (lane < after)
            pivot = base + lax.broadcasted_iota(jnp.int32, (STRIP, 1), 0)
            halves = split(jnp.where(own & (lane > pivot), 0.0, strip))
            turned = split(strip[:, after:].T)
            trailing = jnp.where(own, 0.0, tile_ref[after:, :])
            tile_ref[after:, :] = trailing - product(turned, halves)
    row = lax.broadcasted_iota(jnp.int32, (B, B), 0)
    col = lax.broadcasted_iota(jnp.int32, (B, B), 1)
    return jnp.where(row >= col, tile_ref[...], 0.0)


def tile_at(index):
    return pl.ds(pl.multiple_of(index * B, B), B)


def compute_kernel(panels, place, among_panels, among_cols, among_rows, block, complement, factor, solved, work, total, tile):
    cols_here = complement.shape[1]
    col_tiles = cols_here // B
    tiles = K + col_tiles + 1
    row_tile = place[0]
    first_col = place[1]
    for p in range(K):
        for k in range(SHARES):
            rows = slice(p * B + k * SHARE, p * B + (k + 1) * SHARE)
            work[rows, p * B : K * B] = among_panels[k, p, :, p * B :]
            work[rows, K * B : K * B + cols_here] = among_cols[k, p, :, :cols_here]
            work[rows, K * B + cols_here : tiles * B] = among_rows[k, p]
            work[rows, tiles * B :] = among_cols[k, p, :, cols_here:]
    total[...] = block[...]
    tail = pl.ds(tiles * B, SIDES)

    def step(p, gone):
        target = panels[p]
        tile[...] = work[tile_at(p), tile_at(p)]
        inverse = split(invert_factor(tile))

        def scale_tile(c, _):
            work[tile_at(p), tile_at(c)] = product(inverse, split(work[tile_at(p), tile_at(c)]))
            return 0

        lax.fori_loop(p + 1, tiles, scale_tile, 0)
        side = product(inverse, split(work[tile_at(p), tail]))
        side_halves = split(side)

        def update_row(q, _):
            turned = split(work[tile_at(p), tile_at(q)].T)

            def update_tile(c, _):
                work[tile_at(q), tile_at(c)] -= product(turned, split(work[tile_at(p), tile_at(c)]))
                return 0

            lax.fori_loop(q, tiles, update_tile, 0)
            work[tile_at(q), tail] -= product(turned, side_halves)
            return 0

        lax.fori_loop(p + 1, K, update_row, 0)
        mine = work[tile_at(p), pl.ds((tiles - 1) * B, B)].T * (1.0 - gone)
        factor[:, tile_at(p)] = mine
        turned = split(mine)
        for c in range(col_tiles):
            part = work[tile_at(p), pl.ds((K + c) * B, B)]
            total[:, c * B : (c + 1) * B] -= product(turned, split(part))
        rest = total[:, cols_here:] - product(turned, side_halves)
        total[:, cols_here:] = jnp.where(row_tile == target, side, rest)
        return jnp.where(row_tile == target, 1.0, gone)

    gone = lax.fori_loop(0, K, step, jnp.float32(0.0))
    for c in range(col_tiles):
        keep = 1.0 - gone
        for p in range(K):
            keep = jnp.where(panels[p] == first_col + c, 0.0, keep)
        complement[:, c * B : (c + 1) * B] = total[:, c * B : (c + 1) * B] * keep
    solved[...] = total[:, cols_here:].T


def compute(panels, place, shares, block):
    rows_here, cols_here = block.shape[0], block.shape[1] - SIDES
    vmem = pl.BlockSpec(memory_space=pltpu.VMEM)
    smem = pl.BlockSpec(memory_space=pltpu.SMEM)
    return pl.pallas_call(
        compute_kernel,
        out_shape=(
            jax.ShapeDtypeStruct((rows_here, cols_here), jnp.float32),
            jax.ShapeDtypeStruct((rows_here, K * B), jnp.float32),
            jax.ShapeDtypeStruct((SIDES, rows_here), jnp.float32),
        ),
        in_specs=[smem, smem, vmem, vmem, vmem, vmem],
        out_specs=(vmem, vmem, vmem),
        scratch_shapes=[
            pltpu.VMEM((K * B, K * B + cols_here + B + SIDES), jnp.float32),
            pltpu.VMEM(block.shape, jnp.float32),
            pltpu.VMEM((B, B), jnp.float32),
        ],
        compiler_params=pltpu.CompilerParams(vmem_limit_bytes=56 * 1024 * 1024),
        cost_estimate=pl.CostEstimate(flops=10**10, bytes_accessed=10**7, transcendentals=0),
    )(panels, place, *shares, block)


def gather_kernel(
    panels, block, among_panels, among_cols, among_rows, pieces, slabs,
    piece_send, piece_recv, slab_send, slab_recv, col_send, col_recv, colf_send, colf_recv,
    row_send, row_recv, pan_send, pan_recv, panf_send, panf_recv,
):
    me = lax.axis_index("row")
    layer = lax.axis_index("col")
    layers = slabs.shape[0] // 2
    chips = SHARES // 2
    chip = me // 2
    core = me % 2
    other = chip * 2 + (1 - core)
    cols_here = block.shape[1] - SIDES

    barrier = pltpu.get_barrier_semaphore()
    for o in range(1, SHARES):
        pl.semaphore_signal(barrier, inc=1, device_id={"row": (me + o) % SHARES}, device_id_type=pl.DeviceIdType.MESH)
    for o in range(1, layers):
        pl.semaphore_signal(barrier, inc=1, device_id={"col": (layer + o) % layers}, device_id_type=pl.DeviceIdType.MESH)
    pl.semaphore_wait(barrier, SHARES - 1 + layers - 1)

    def send(source, target, sends, recvs, where):
        copy = pltpu.make_async_remote_copy(
            src_ref=source, dst_ref=target, send_sem=sends, recv_sem=recvs,
            device_id=where, device_id_type=pl.DeviceIdType.MESH,
        )
        copy.start()
        return copy

    def share_of(index):
        return pl.ds(pl.multiple_of(index * SHARE, SHARE), SHARE)

    dealt = []
    for o in range(1, SHARES):
        peer = (me + o) % SHARES
        dealt.append(
            send(block.at[share_of(peer)], pieces.at[me], piece_send.at[o], piece_recv.at[o], {"row": peer})
        )
    pieces[me] = block[share_of(me), :]
    for copy in dealt:
        copy.wait_recv()

    for s in range(K):
        packed = pieces[panels[s]]
        among_cols[me, s] = packed
        for c in range(2):
            slabs[2 * layer + c, s] = packed[:, c * B : (c + 1) * B]
    mine = slabs.at[pl.ds(2 * layer, 2)]
    spread = [
        send(mine, mine, slab_send.at[o], slab_recv.at[o], {"col": (layer + o) % layers})
        for o in range(1, layers)
    ]
    col_share = among_cols.at[me]
    cols = [
        send(col_share, col_share, col_send.at[o], col_recv.at[o], {"row": ((chip + o) % chips) * 2 + core})
        for o in range(1, chips)
    ]
    passed = [send(col_share, col_share, colf_send.at[0], colf_recv.at[0], {"row": other})]
    for copy in spread:
        copy.wait_recv()

    for s in range(K):
        for q in range(s, K):
            among_panels[me, s, :, q * B : (q + 1) * B] = slabs[panels[q], s]
    pans = []
    for o in range(1, chips):
        for s in range(K):
            part = among_panels.at[me, s, :, pl.ds(s * B, (K - s) * B)]
            pans.append(
                send(part, part, pan_send.at[o, s], pan_recv.at[o, s], {"row": ((chip + o) % chips) * 2 + core})
            )
    for s in range(K):
        part = among_panels.at[me, s, :, pl.ds(s * B, (K - s) * B)]
        passed.append(send(part, part, panf_send.at[0, s], panf_recv.at[0, s], {"row": other}))
    rows = []
    for o in range(1, SHARES):
        peer = (me + o) % SHARES
        rows.append(send(slabs.at[peer], among_rows.at[me], row_send.at[o], row_recv.at[o], {"row": peer}))
    among_rows[me] = slabs[me]

    for o in range(1, chips):
        cols[o - 1].wait_recv()
        share = among_cols.at[((chip + chips - o) % chips) * 2 + core]
        passed.append(send(share, share, colf_send.at[o], colf_recv.at[o], {"row": other}))
    for o in range(1, chips):
        for s in range(K):
            pans[(o - 1) * K + s].wait_recv()
            part = among_panels.at[((chip + chips - o) % chips) * 2 + core, s, :, pl.ds(s * B, (K - s) * B)]
            passed.append(send(part, part, panf_send.at[o, s], panf_recv.at[o, s], {"row": other}))
    for copy in passed + rows:
        copy.wait_recv()
    for copy in dealt + spread + cols + pans + rows + passed:
        copy.wait_send()


def gather_by_copies(panels, block, layers):
    cols_here = block.shape[1] - SIDES
    vmem = pl.BlockSpec(memory_space=pltpu.VMEM)
    smem = pl.BlockSpec(memory_space=pltpu.SMEM)
    chips = SHARES // 2
    dma = pltpu.SemaphoreType.DMA
    return pl.pallas_call(
        gather_kernel,
        out_shape=(
            jax.ShapeDtypeStruct((SHARES, K, SHARE, K * B), jnp.float32),
            jax.ShapeDtypeStruct((SHARES, K, SHARE, cols_here + SIDES), jnp.float32),
            jax.ShapeDtypeStruct((SHARES, K, SHARE, B), jnp.float32),
        ),
        in_specs=[smem, vmem],
        out_specs=(vmem, vmem, vmem),
        scratch_shapes=[
            pltpu.VMEM((SHARES, SHARE, cols_here + SIDES), jnp.float32),
            pltpu.VMEM((2 * layers, K, SHARE, B), jnp.float32),
        ]
        + [dma((SHARES,))] * 2 + [dma((layers,))] * 2 + [dma((chips,))] * 4
        + [dma((SHARES,))] * 2 + [dma((chips, K))] * 4,
        compiler_params=pltpu.CompilerParams(
            collective_id=0, has_side_effects=True, vmem_limit_bytes=56 * 1024 * 1024
        ),
    )(panels, block)


def gather_by_sums(panels, row_tile, first_col, block):
    cols_here = block.shape[1] - SIDES
    col_tiles = cols_here // B
    mine = (panels == row_tile).astype(jnp.float32)
    rows = lax.psum((mine[:, None, None] * block[None]).reshape(K * B, -1), "row")
    parts = []
    for wanted in [panels[p] for p in range(K)] + [row_tile]:
        local = wanted - first_col
        held = (local >= 0) & (local < col_tiles)
        part = lax.dynamic_slice_in_dim(rows, jnp.clip(local, 0, col_tiles - 1) * B, B, 1)
        parts.append(jnp.where(held, part, 0.0))
    spread = lax.psum(jnp.concatenate(parts, axis=1), "col")
    return [
        part.reshape(K, SHARES, SHARE, -1).transpose(1, 0, 2, 3)
        for part in (spread[:, : K * B], rows, spread[:, K * B :])
    ]


def on_device(paired, layers, covariance, panels, observed, drift_basis):
    rows_here, cols_here = covariance.shape
    row_tile = lax.axis_index("row")
    first_col = lax.axis_index("col") * (cols_here // B)
    drifts = drift_basis.shape[0]
    sides = jnp.concatenate(
        [observed[None, :], drift_basis, jnp.zeros((SIDES - 1 - drifts, rows_here), jnp.float32)], axis=0
    )
    block = jnp.concatenate([covariance, sides.T], axis=1)
    if paired:
        shares = gather_by_copies(panels, block, layers)
    else:
        shares = gather_by_sums(panels, row_tile, first_col, block)
    place = jnp.stack([row_tile, first_col]).astype(jnp.int32)
    complement, factor, solved = compute(panels, place, shares, block)
    return complement, factor, solved[0], solved[1 : 1 + drifts]


def solution(mesh):
    row, col = mesh.shape["row"], mesh.shape["col"]
    paired = row == SHARES and 2 * col == row
    return jax.shard_map(
        functools.partial(on_device, paired, col),
        mesh=mesh,
        in_specs=(P("row", "col"), P(), P("row"), P(None, "row")),
        out_specs=(P("row", "col"), P("row", None), P("row"), P(None, "row")),
        check_vma=False,
    )
```

```python
import functools

import jax
import jax.numpy as jnp
from jax import lax
from jax.experimental import pallas as pl
from jax.experimental.pallas import tpu as pltpu
from jax.sharding import PartitionSpec as P

B = 256
K = 4
STRIP = 32
GROUP = 8
LANES = 128
SIDES = 128
SHARES = 8
SHARE = B // SHARES
PARTS = ((0, 1), (1, K))


def split(value):
    high = value.astype(jnp.bfloat16)
    low = (value - high.astype(jnp.float32)).astype(jnp.bfloat16)
    return high, low


def product(left, right, dims=((1,), (0,))):
    one = functools.partial(
        lax.dot_general,
        dimension_numbers=(dims, ((), ())),
        preferred_element_type=jnp.float32,
    )
    return one(left[0], right[0]) + (one(left[0], right[1]) + one(left[1], right[0]))


def eliminate_strip(strip, base):
    halves = [strip[:, h * LANES : (h + 1) * LANES] for h in range(B // LANES)]
    done = [[] for _ in halves]
    lane = lax.broadcasted_iota(jnp.int32, (1, LANES), 1)
    for group in range(STRIP // GROUP):
        rows = STRIP - group * GROUP
        row = lax.broadcasted_iota(jnp.int32, (rows, 1), 0)
        first = base + group * GROUP
        home, where = first // LANES, first % LANES
        columns = [
            jnp.broadcast_to(halves[home][:, where + c : where + c + 1], (rows, LANES))
            for c in range(GROUP)
        ]
        for c in range(GROUP):
            scale = lax.rsqrt(columns[c][c : c + 1, :])
            below = row > c
            factor = jnp.where(below, columns[c] * scale, 0.0)
            for d in range(c + 1, GROUP):
                columns[d] = columns[d] - factor * (columns[d][c : c + 1, :] * scale)
            for h in range(len(halves)):
                pivot = halves[h][c : c + 1, :] * scale
                rest = halves[h]
                if h == home:
                    here = lane == where + c
                    pivot = jnp.where(here, scale, pivot)
                    rest = jnp.where(here & below, 0.0, rest)
                halves[h] = jnp.where(row == c, pivot, rest - factor * pivot)
        for h in range(len(halves)):
            done[h].append(halves[h][:GROUP])
            halves[h] = halves[h][GROUP:]
    return jnp.concatenate([jnp.concatenate(part, axis=0) for part in done], axis=1)


def invert_factor(tile_ref, halfway):
    lane = lax.broadcasted_iota(jnp.int32, (1, B), 1)
    for base in range(0, B, STRIP):
        if base == B // 2:
            halfway()
        strip = eliminate_strip(tile_ref[base : base + STRIP, :], base)
        tile_ref[base : base + STRIP, :] = strip
        after = base + STRIP
        if after < B:
            own = (lane >= base) & (lane < after)
            pivot = base + lax.broadcasted_iota(jnp.int32, (STRIP, 1), 0)
            halves = split(jnp.where(own & (lane > pivot), 0.0, strip))
            turned = split(strip[:, after:].T)
            trailing = jnp.where(own, 0.0, tile_ref[after:, :])
            tile_ref[after:, :] = trailing - product(turned, halves)
    row = lax.broadcasted_iota(jnp.int32, (B, B), 0)
    col = lax.broadcasted_iota(jnp.int32, (B, B), 1)
    return jnp.where(row >= col, tile_ref[...], 0.0)


def tile_at(index):
    return pl.ds(pl.multiple_of(index * B, B), B)


def run_steps(panels, shares, outs, work, total, tile, halfway, arrived):
    among_panels, among_cols, among_rows = shares
    complement, factor, data, drift = outs
    cols_here = complement.shape[1]
    drifts = drift.shape[0]
    col_tiles = cols_here // B
    tiles = K + col_tiles + 1
    row_tile = lax.axis_index("row")
    first_col = lax.axis_index("col") * col_tiles
    tail = pl.ds(tiles * B, SIDES)
    tile[...] = among_panels[:, 0, :, :B].reshape(B, B)

    def at_first(p, action):
        def run():
            pl.when(p == 0)(action)

        return run

    def assemble():
        arrived()
        for p in range(K):
            for k in range(SHARES):
                rows = slice(p * B + k * SHARE, p * B + (k + 1) * SHARE)
                work[rows, p * B : K * B] = among_panels[k, p, :, p * B :]
                work[rows, K * B : K * B + cols_here] = among_cols[k, p, :, :cols_here]
                work[rows, K * B + cols_here : tiles * B] = among_rows[k, p]
                work[rows, tiles * B :] = among_cols[k, p, :, cols_here:]

    def step(p, gone):
        target = panels[p]
        inverse = split(invert_factor(tile, at_first(p, halfway)))
        at_first(p, assemble)()

        def scale_tile(c, _):
            work[tile_at(p), tile_at(c)] = product(inverse, split(work[tile_at(p), tile_at(c)]))
            return 0

        lax.fori_loop(p + 1, tiles, scale_tile, 0)
        side = product(inverse, split(work[tile_at(p), tail]))
        side_halves = split(side)

        def update_row(q, _):
            turned = split(work[tile_at(p), tile_at(q)].T)

            def update_tile(c, _):
                work[tile_at(q), tile_at(c)] -= product(turned, split(work[tile_at(p), tile_at(c)]))
                return 0

            lax.fori_loop(q, tiles, update_tile, 0)
            work[tile_at(q), tail] -= product(turned, side_halves)
            return 0

        lax.fori_loop(p + 1, K, update_row, 0)
        mine = work[tile_at(p), pl.ds((tiles - 1) * B, B)].T * (1.0 - gone)
        factor[:, tile_at(p)] = mine
        turned = split(mine)
        for c in range(col_tiles):
            part = work[tile_at(p), pl.ds((K + c) * B, B)]
            total[:, c * B : (c + 1) * B] -= product(turned, split(part))
        rest = total[:, cols_here:] - product(turned, side_halves)
        total[:, cols_here:] = jnp.where(row_tile == target, side, rest)
        following = jnp.minimum(p + 1, K - 1)
        tile[...] = work[tile_at(following), tile_at(following)]
        return jnp.where(row_tile == target, 1.0, gone)

    gone = lax.fori_loop(0, K, step, jnp.float32(0.0))
    for c in range(col_tiles):
        keep = 1.0 - gone
        for p in range(K):
            keep = jnp.where(panels[p] == first_col + c, 0.0, keep)
        complement[:, c * B : (c + 1) * B] = total[:, c * B : (c + 1) * B] * keep
    solved = total[:, cols_here:].T
    drift[...] = solved[:drifts]
    data[...] = solved[drifts : drifts + 1]


def stack_block(covariance, data, drift, total):
    cols_here = covariance.shape[1]
    filler = jnp.zeros((SIDES - drift.shape[0] - 1, B), jnp.float32)
    total[:, :cols_here] = covariance[...]
    total[:, cols_here:] = jnp.concatenate([drift[...], data[...], filler], axis=0).T


def local_kernel(panels, covariance, data, drift, *refs):
    shares, outs, (work, total, tile) = refs[:3], refs[3:7], refs[7:]
    stack_block(covariance, data, drift, total)
    run_steps(panels, shares, outs, work, total, tile, lambda: None, lambda: None)


def copies_kernel(panels, covariance, data, drift, *refs):
    outs, (work, total, tile), shares, (pieces, *slabs) = refs[:4], refs[4:7], refs[7:10], refs[10:13]
    (
        piece_send, piece_recv, slab_send, slab_recv, col_send, col_recv, colf_send, colf_recv,
        row_send, row_recv, pan_send, pan_recv, panf_send, panf_recv,
    ) = refs[13:]
    among_panels, among_cols, among_rows = shares
    me = lax.axis_index("row")
    layer = lax.axis_index("col")
    layers = slabs[0].shape[0] // 2
    chips = SHARES // 2
    chip = me // 2
    core = me % 2
    other = chip * 2 + (1 - core)

    barrier = pltpu.get_barrier_semaphore()
    for o in range(1, SHARES):
        pl.semaphore_signal(barrier, inc=1, device_id={"row": (me + o) % SHARES}, device_id_type=pl.DeviceIdType.MESH)
    for o in range(1, layers):
        pl.semaphore_signal(barrier, inc=1, device_id={"col": (layer + o) % layers}, device_id_type=pl.DeviceIdType.MESH)
    pl.semaphore_wait(barrier, SHARES - 1 + layers - 1)

    stack_block(covariance, data, drift, total)

    def send(source, target, sends, recvs, where):
        copy = pltpu.make_async_remote_copy(
            src_ref=source, dst_ref=target, send_sem=sends, recv_sem=recvs,
            device_id=where, device_id_type=pl.DeviceIdType.MESH,
        )
        copy.start()
        return copy

    def share_of(index):
        return pl.ds(pl.multiple_of(index * SHARE, SHARE), SHARE)

    def twin(o):
        return {"row": ((chip + o) % chips) * 2 + core}

    def twin_share(o):
        return ((chip + chips - o) % chips) * 2 + core

    def panel_part(share, s):
        return among_panels.at[share, s, :, pl.ds(s * B, (K - s) * B)]

    dealt = []
    for o in range(1, SHARES):
        peer = (me + o) % SHARES
        dealt.append(
            send(total.at[share_of(peer)], pieces.at[me], piece_send.at[o], piece_recv.at[o], {"row": peer})
        )
    pieces[me] = total[share_of(me), :]
    for copy in dealt:
        copy.wait_recv()

    spread = []
    for part, (low, high) in enumerate(PARTS):
        for s in range(low, high):
            packed = pieces[panels[s]]
            among_cols[me, s] = packed
            for c in range(2):
                slabs[part][2 * layer + c, s - low] = packed[:, c * B : (c + 1) * B]
        mine = slabs[part].at[pl.ds(2 * layer, 2)]
        spread.append([
            send(mine, mine, slab_send.at[o, part], slab_recv.at[o, part], {"col": (layer + o) % layers})
            for o in range(1, layers)
        ])
    col_share = among_cols.at[me]
    cols = [send(col_share, col_share, col_send.at[o], col_recv.at[o], twin(o)) for o in range(1, chips)]
    passed = [send(col_share, col_share, colf_send.at[0], colf_recv.at[0], {"row": other})]

    pans, firsts, laters = [], [], []
    for s in range(K):
        for part, (low, high) in enumerate(PARTS):
            if s == low:
                for copy in spread[part]:
                    copy.wait_recv()
            if low <= s < high:
                for q in range(s, K):
                    among_panels[me, s, :, q * B : (q + 1) * B] = slabs[part][panels[q], s - low]
        part = panel_part(me, s)
        pans.append([send(part, part, pan_send.at[o, s], pan_recv.at[o, s], twin(o)) for o in range(1, chips)])
        (laters if s else firsts).append(send(part, part, panf_send.at[0, s], panf_recv.at[0, s], {"row": other}))
    rows = []
    for o in range(1, SHARES):
        peer = (me + o) % SHARES
        for part, (low, high) in enumerate(PARTS):
            source = slabs[part].at[peer]
            target = among_rows.at[me, pl.ds(low, high - low)]
            rows.append(send(source, target, row_send.at[o, part], row_recv.at[o, part], {"row": peer}))
    for part, (low, high) in enumerate(PARTS):
        among_rows[me, low:high] = slabs[part][me]

    def pass_panels(o, s):
        pans[s][o - 1].wait_recv()
        part = panel_part(twin_share(o), s)
        return send(part, part, panf_send.at[o, s], panf_recv.at[o, s], {"row": other})

    firsts += [pass_panels(o, 0) for o in range(1, chips)]
    for o in range(1, chips):
        cols[o - 1].wait_recv()
        share = among_cols.at[twin_share(o)]
        passed.append(send(share, share, colf_send.at[o], colf_recv.at[o], {"row": other}))
    for copy in firsts:
        copy.wait_recv()
    for copy in dealt:
        copy.wait_send()

    def halfway():
        for s in range(1, K):
            for o in range(1, chips):
                pass_panels(o, s)

    def arrived():
        late = []
        for s in range(1, K):
            for o in range(1, chips):
                part = panel_part(twin_share(o), s)
                late.append(
                    pltpu.make_async_remote_copy(
                        src_ref=part, dst_ref=part, send_sem=panf_send.at[o, s], recv_sem=panf_recv.at[o, s],
                        device_id={"row": other}, device_id_type=pl.DeviceIdType.MESH,
                    )
                )
        for copy in late + laters + passed + rows:
            copy.wait_recv()
        for group in [cols, rows, passed, firsts, laters, late] + pans + spread:
            for copy in group:
                copy.wait_send()

    run_steps(panels, shares, outs, work, total, tile, halfway, arrived)


def call(kernel, panels, covariance, data, drift, shares, scratch, **params):
    rows_here, cols_here = covariance.shape
    vmem = pl.BlockSpec(memory_space=pltpu.VMEM)
    smem = pl.BlockSpec(memory_space=pltpu.SMEM)
    return pl.pallas_call(
        kernel,
        out_shape=(
            jax.ShapeDtypeStruct((rows_here, cols_here), jnp.float32),
            jax.ShapeDtypeStruct((rows_here, K * B), jnp.float32),
            jax.ShapeDtypeStruct(data.shape, jnp.float32),
            jax.ShapeDtypeStruct(drift.shape, jnp.float32),
        ),
        in_specs=[smem] + [vmem] * (3 + len(shares)),
        out_specs=(vmem,) * 4,
        scratch_shapes=[
            pltpu.VMEM((K * B, K * B + cols_here + B + SIDES), jnp.float32),
            pltpu.VMEM((rows_here, cols_here + SIDES), jnp.float32),
            pltpu.VMEM((B, B), jnp.float32),
        ]
        + scratch,
        compiler_params=pltpu.CompilerParams(vmem_limit_bytes=56 * 1024 * 1024, **params),
        cost_estimate=pl.CostEstimate(flops=10**10, bytes_accessed=10**7, transcendentals=0),
    )(panels, covariance, data, drift, *shares)


def by_copies(layers, panels, covariance, data, drift):
    cols_here = covariance.shape[1]
    chips = SHARES // 2
    dma = pltpu.SemaphoreType.DMA
    scratch = [
        pltpu.VMEM((SHARES, K, SHARE, K * B), jnp.float32),
        pltpu.VMEM((SHARES, K, SHARE, cols_here + SIDES), jnp.float32),
        pltpu.VMEM((SHARES, K, SHARE, B), jnp.float32),
        pltpu.VMEM((SHARES, SHARE, cols_here + SIDES), jnp.float32),
    ]
    scratch += [pltpu.VMEM((2 * layers, high - low, SHARE, B), jnp.float32) for low, high in PARTS]
    scratch += [dma((SHARES,))] * 2 + [dma((layers, len(PARTS)))] * 2 + [dma((chips,))] * 4
    scratch += [dma((SHARES, len(PARTS)))] * 2 + [dma((chips, K))] * 4
    return call(
        copies_kernel, panels, covariance, data, drift, [], scratch, collective_id=0, has_side_effects=True
    )


def gather_by_sums(panels, row_tile, first_col, block):
    cols_here = block.shape[1] - SIDES
    col_tiles = cols_here // B
    mine = (panels == row_tile).astype(jnp.float32)
    rows = lax.psum((mine[:, None, None] * block[None]).reshape(K * B, -1), "row")
    parts = []
    for wanted in [panels[p] for p in range(K)] + [row_tile]:
        local = wanted - first_col
        held = (local >= 0) & (local < col_tiles)
        part = lax.dynamic_slice_in_dim(rows, jnp.clip(local, 0, col_tiles - 1) * B, B, 1)
        parts.append(jnp.where(held, part, 0.0))
    spread = lax.psum(jnp.concatenate(parts, axis=1), "col")
    return [
        part.reshape(K, SHARES, SHARE, -1).transpose(1, 0, 2, 3)
        for part in (spread[:, : K * B], rows, spread[:, K * B :])
    ]


def on_device(paired, layers, covariance, panels, observed, drift_basis):
    cols_here = covariance.shape[1]
    data = observed[None, :]
    if paired:
        complement, factor, data, drift = by_copies(layers, panels, covariance, data, drift_basis)
        return complement, factor, data[0], drift
    filler = jnp.zeros((SIDES - 1 - drift_basis.shape[0], B), jnp.float32)
    sides = jnp.concatenate([drift_basis, data, filler], axis=0)
    block = jnp.concatenate([covariance, sides.T], axis=1)
    first_col = lax.axis_index("col") * (cols_here // B)
    shares = gather_by_sums(panels, lax.axis_index("row"), first_col, block)
    complement, factor, data, drift = call(
        local_kernel, panels, covariance, data, drift_basis, shares, []
    )
    return complement, factor, data[0], drift


def solution(mesh):
    row, col = mesh.shape["row"], mesh.shape["col"]
    paired = row == SHARES and 2 * col == row
    return jax.shard_map(
        functools.partial(on_device, paired, col),
        mesh=mesh,
        in_specs=(P("row", "col"), P(), P("row"), P(None, "row")),
        out_specs=(P("row", "col"), P("row", None), P("row"), P(None, "row")),
        check_vma=False,
    )
```

```python
import functools

import jax
import jax.numpy as jnp
from jax import lax
from jax.experimental import pallas as pl
from jax.experimental.pallas import tpu as pltpu
from jax.sharding import PartitionSpec as P

B = 256
K = 4
STRIP = 32
GROUP = 8
LANES = 128
SIDES = 128
SHARES = 8
SHARE = B // SHARES
PARTS = ((0, 1), (1, K))


def split(value):
    high = value.astype(jnp.bfloat16)
    low = (value - high.astype(jnp.float32)).astype(jnp.bfloat16)
    return high, low


def product(left, right, dims=((1,), (0,))):
    one = functools.partial(
        lax.dot_general,
        dimension_numbers=(dims, ((), ())),
        preferred_element_type=jnp.float32,
    )
    return one(left[0], right[0]) + (one(left[0], right[1]) + one(left[1], right[0]))


def eliminate_strip(strip, base):
    halves = [strip[:, h * LANES : (h + 1) * LANES] for h in range(B // LANES)]
    done = [[] for _ in halves]
    lane = lax.broadcasted_iota(jnp.int32, (1, LANES), 1)
    for group in range(STRIP // GROUP):
        rows = STRIP - group * GROUP
        row = lax.broadcasted_iota(jnp.int32, (rows, 1), 0)
        first = base + group * GROUP
        home, where = first // LANES, first % LANES
        columns = [
            jnp.broadcast_to(halves[home][:, where + c : where + c + 1], (rows, LANES))
            for c in range(GROUP)
        ]
        for c in range(GROUP):
            scale = lax.rsqrt(columns[c][c : c + 1, :])
            below = row > c
            factor = jnp.where(below, columns[c] * scale, 0.0)
            for d in range(c + 1, GROUP):
                columns[d] = columns[d] - factor * (columns[d][c : c + 1, :] * scale)
            for h in range(len(halves)):
                pivot = halves[h][c : c + 1, :] * scale
                rest = halves[h]
                if h == home:
                    here = lane == where + c
                    pivot = jnp.where(here, scale, pivot)
                    rest = jnp.where(here & below, 0.0, rest)
                halves[h] = jnp.where(row == c, pivot, rest - factor * pivot)
        for h in range(len(halves)):
            done[h].append(halves[h][:GROUP])
            halves[h] = halves[h][GROUP:]
    return jnp.concatenate([jnp.concatenate(part, axis=0) for part in done], axis=1)


def invert_factor(tile_ref, halfway):
    lane = lax.broadcasted_iota(jnp.int32, (1, B), 1)
    for base in range(0, B, STRIP):
        if base == B // 2:
            halfway()
        strip = eliminate_strip(tile_ref[base : base + STRIP, :], base)
        tile_ref[base : base + STRIP, :] = strip
        after = base + STRIP
        if after < B:
            own = (lane >= base) & (lane < after)
            pivot = base + lax.broadcasted_iota(jnp.int32, (STRIP, 1), 0)
            halves = split(jnp.where(own & (lane > pivot), 0.0, strip))
            turned = split(strip[:, after:].T)
            trailing = jnp.where(own, 0.0, tile_ref[after:, :])
            tile_ref[after:, :] = trailing - product(turned, halves)
    row = lax.broadcasted_iota(jnp.int32, (B, B), 0)
    col = lax.broadcasted_iota(jnp.int32, (B, B), 1)
    return jnp.where(row >= col, tile_ref[...], 0.0)


def tile_at(index):
    return pl.ds(pl.multiple_of(index * B, B), B)


def run_steps(panels, shares, outs, work, total, tile, halfway, arrived, rows_arrived):
    among_panels, among_cols, among_rows = shares
    complement, factor, data, drift = outs
    cols_here = complement.shape[1]
    drifts = drift.shape[0]
    col_tiles = cols_here // B
    tiles = K + col_tiles + 1
    row_tile = lax.axis_index("row")
    first_col = lax.axis_index("col") * col_tiles
    tail = pl.ds(tiles * B, SIDES)
    tile[...] = among_panels[:, 0, :, :B].reshape(B, B)

    def at_first(p, action):
        def run():
            pl.when(p == 0)(action)

        return run

    def assemble():
        arrived()
        for p in range(K):
            for k in range(SHARES):
                rows = slice(p * B + k * SHARE, p * B + (k + 1) * SHARE)
                work[rows, p * B : K * B] = among_panels[k, p, :, p * B :]
                work[rows, K * B : K * B + cols_here] = among_cols[k, p, :, :cols_here]
                work[rows, tiles * B :] = among_cols[k, p, :, cols_here:]

    def assemble_rows():
        rows_arrived()
        for p in range(K):
            for k in range(SHARES):
                rows = slice(p * B + k * SHARE, p * B + (k + 1) * SHARE)
                work[rows, K * B + cols_here : tiles * B] = among_rows[k, p]

    def gone_before(p):
        gone = jnp.float32(0.0)
        for s in range(K):
            gone = jnp.where((panels[s] == row_tile) & (s < p), 1.0, gone)
        return gone

    def rows_step(p):
        own = pl.ds((tiles - 1) * B, B)
        here = product(split(work[tile_at(p), tile_at(p)]), split(work[tile_at(p), own]))
        here_halves = split(here)

        def update_row(q, _):
            work[tile_at(q), own] -= product(split(work[tile_at(p), tile_at(q)].T), here_halves)
            return 0

        lax.fori_loop(p + 1, K, update_row, 0)
        mine = here.T * (1.0 - gone_before(p))
        factor[:, tile_at(p)] = mine
        turned = split(mine)
        for c in range(col_tiles):
            part = work[tile_at(p), pl.ds((K + c) * B, B)]
            total[:, c * B : (c + 1) * B] -= product(turned, split(part))
        side = work[tile_at(p), tail]
        rest = total[:, cols_here:] - product(turned, split(side))
        total[:, cols_here:] = jnp.where(row_tile == panels[p], side, rest)

    def step(p, _):
        exact = invert_factor(tile, at_first(p, halfway))
        inverse = split(exact)
        at_first(p, assemble)()
        work[tile_at(p), tile_at(p)] = exact

        def scale_tile(c, _):
            work[tile_at(p), tile_at(c)] = product(inverse, split(work[tile_at(p), tile_at(c)]))
            return 0

        lax.fori_loop(p + 1, tiles - 1, scale_tile, 0)
        side = product(inverse, split(work[tile_at(p), tail]))
        side_halves = split(side)
        work[tile_at(p), tail] = side

        def update_row(q, _):
            turned = split(work[tile_at(p), tile_at(q)].T)

            def update_tile(c, _):
                work[tile_at(q), tile_at(c)] -= product(turned, split(work[tile_at(p), tile_at(c)]))
                return 0

            lax.fori_loop(q, tiles - 1, update_tile, 0)
            work[tile_at(q), tail] -= product(turned, side_halves)
            return 0

        lax.fori_loop(p + 1, K, update_row, 0)

        def lagging():
            pl.when(p == 1)(assemble_rows)
            rows_step(p - 1)

        pl.when(p > 0)(lagging)
        following = jnp.minimum(p + 1, K - 1)
        tile[...] = work[tile_at(following), tile_at(following)]
        return 0

    lax.fori_loop(0, K, step, 0)
    rows_step(K - 1)
    gone = gone_before(K)
    for c in range(col_tiles):
        keep = 1.0 - gone
        for p in range(K):
            keep = jnp.where(panels[p] == first_col + c, 0.0, keep)
        complement[:, c * B : (c + 1) * B] = total[:, c * B : (c + 1) * B] * keep
    solved = total[:, cols_here:].T
    drift[...] = solved[:drifts]
    data[...] = solved[drifts : drifts + 1]


def stack_block(covariance, data, drift, total):
    cols_here = covariance.shape[1]
    filler = jnp.zeros((SIDES - drift.shape[0] - 1, B), jnp.float32)
    total[:, :cols_here] = covariance[...]
    total[:, cols_here:] = jnp.concatenate([drift[...], data[...], filler], axis=0).T


def local_kernel(panels, covariance, data, drift, *refs):
    shares, outs, (work, total, tile) = refs[:3], refs[3:7], refs[7:]
    stack_block(covariance, data, drift, total)
    run_steps(panels, shares, outs, work, total, tile, *[lambda: None] * 3)


def copies_kernel(panels, covariance, data, drift, *refs):
    outs, (work, total, tile), shares, (pieces, *slabs) = refs[:4], refs[4:7], refs[7:10], refs[10:13]
    (
        piece_send, piece_recv, slab_send, slab_recv, col_send, col_recv, colf_send, colf_recv,
        row_send, row_recv, pan_send, pan_recv, panf_send, panf_recv,
    ) = refs[13:]
    among_panels, among_cols, among_rows = shares
    me = lax.axis_index("row")
    layer = lax.axis_index("col")
    layers = slabs[0].shape[0] // 2
    chips = SHARES // 2
    chip = me // 2
    core = me % 2
    other = chip * 2 + (1 - core)

    barrier = pltpu.get_barrier_semaphore()
    for o in range(1, SHARES):
        pl.semaphore_signal(barrier, inc=1, device_id={"row": (me + o) % SHARES}, device_id_type=pl.DeviceIdType.MESH)
    for o in range(1, layers):
        pl.semaphore_signal(barrier, inc=1, device_id={"col": (layer + o) % layers}, device_id_type=pl.DeviceIdType.MESH)
    pl.semaphore_wait(barrier, SHARES - 1 + layers - 1)

    stack_block(covariance, data, drift, total)

    def send(source, target, sends, recvs, where):
        copy = pltpu.make_async_remote_copy(
            src_ref=source, dst_ref=target, send_sem=sends, recv_sem=recvs,
            device_id=where, device_id_type=pl.DeviceIdType.MESH,
        )
        copy.start()
        return copy

    def share_of(index):
        return pl.ds(pl.multiple_of(index * SHARE, SHARE), SHARE)

    def twin(o):
        return {"row": ((chip + o) % chips) * 2 + core}

    def twin_share(o):
        return ((chip + chips - o) % chips) * 2 + core

    def panel_part(share, s):
        return among_panels.at[share, s, :, pl.ds(s * B, (K - s) * B)]

    dealt = []
    for o in range(1, SHARES):
        peer = (me + o) % SHARES
        dealt.append(
            send(total.at[share_of(peer)], pieces.at[me], piece_send.at[o], piece_recv.at[o], {"row": peer})
        )
    pieces[me] = total[share_of(me), :]
    for copy in dealt:
        copy.wait_recv()

    spread = []
    for part, (low, high) in enumerate(PARTS):
        for s in range(low, high):
            packed = pieces[panels[s]]
            among_cols[me, s] = packed
            for c in range(2):
                slabs[part][2 * layer + c, s - low] = packed[:, c * B : (c + 1) * B]
        mine = slabs[part].at[pl.ds(2 * layer, 2)]
        spread.append([
            send(mine, mine, slab_send.at[o, part], slab_recv.at[o, part], {"col": (layer + o) % layers})
            for o in range(1, layers)
        ])
    col_share = among_cols.at[me]
    cols = [send(col_share, col_share, col_send.at[o], col_recv.at[o], twin(o)) for o in range(1, chips)]
    passed = [send(col_share, col_share, colf_send.at[0], colf_recv.at[0], {"row": other})]

    pans, firsts, laters = [], [], []
    for s in range(K):
        for part, (low, high) in enumerate(PARTS):
            if s == low:
                for copy in spread[part]:
                    copy.wait_recv()
            if low <= s < high:
                for q in range(s, K):
                    among_panels[me, s, :, q * B : (q + 1) * B] = slabs[part][panels[q], s - low]
        part = panel_part(me, s)
        pans.append([send(part, part, pan_send.at[o, s], pan_recv.at[o, s], twin(o)) for o in range(1, chips)])
        (laters if s else firsts).append(send(part, part, panf_send.at[0, s], panf_recv.at[0, s], {"row": other}))
    rows = []
    for o in range(1, SHARES):
        peer = (me + o) % SHARES
        for part, (low, high) in enumerate(PARTS):
            source = slabs[part].at[peer]
            target = among_rows.at[me, pl.ds(low, high - low)]
            rows.append(send(source, target, row_send.at[o, part], row_recv.at[o, part], {"row": peer}))
    for part, (low, high) in enumerate(PARTS):
        among_rows[me, low:high] = slabs[part][me]

    def pass_panels(o, s):
        pans[s][o - 1].wait_recv()
        part = panel_part(twin_share(o), s)
        return send(part, part, panf_send.at[o, s], panf_recv.at[o, s], {"row": other})

    firsts += [pass_panels(o, 0) for o in range(1, chips)]
    for o in range(1, chips):
        cols[o - 1].wait_recv()
        share = among_cols.at[twin_share(o)]
        passed.append(send(share, share, colf_send.at[o], colf_recv.at[o], {"row": other}))
    for copy in firsts:
        copy.wait_recv()
    for copy in dealt:
        copy.wait_send()

    def halfway():
        for s in range(1, K):
            for o in range(1, chips):
                pass_panels(o, s)

    def arrived():
        late = []
        for s in range(1, K):
            for o in range(1, chips):
                part = panel_part(twin_share(o), s)
                late.append(
                    pltpu.make_async_remote_copy(
                        src_ref=part, dst_ref=part, send_sem=panf_send.at[o, s], recv_sem=panf_recv.at[o, s],
                        device_id={"row": other}, device_id_type=pl.DeviceIdType.MESH,
                    )
                )
        for copy in late + laters + passed:
            copy.wait_recv()
        for group in [cols, passed, firsts, laters, late] + pans + spread:
            for copy in group:
                copy.wait_send()

    def rows_arrived():
        for copy in rows:
            copy.wait_recv()
        for copy in rows:
            copy.wait_send()

    run_steps(panels, shares, outs, work, total, tile, halfway, arrived, rows_arrived)


def call(kernel, panels, covariance, data, drift, shares, scratch, **params):
    rows_here, cols_here = covariance.shape
    vmem = pl.BlockSpec(memory_space=pltpu.VMEM)
    smem = pl.BlockSpec(memory_space=pltpu.SMEM)
    return pl.pallas_call(
        kernel,
        out_shape=(
            jax.ShapeDtypeStruct((rows_here, cols_here), jnp.float32),
            jax.ShapeDtypeStruct((rows_here, K * B), jnp.float32),
            jax.ShapeDtypeStruct(data.shape, jnp.float32),
            jax.ShapeDtypeStruct(drift.shape, jnp.float32),
        ),
        in_specs=[smem] + [vmem] * (3 + len(shares)),
        out_specs=(vmem,) * 4,
        scratch_shapes=[
            pltpu.VMEM((K * B, K * B + cols_here + B + SIDES), jnp.float32),
            pltpu.VMEM((rows_here, cols_here + SIDES), jnp.float32),
            pltpu.VMEM((B, B), jnp.float32),
        ]
        + scratch,
        compiler_params=pltpu.CompilerParams(vmem_limit_bytes=56 * 1024 * 1024, **params),
        cost_estimate=pl.CostEstimate(flops=10**10, bytes_accessed=10**7, transcendentals=0),
    )(panels, covariance, data, drift, *shares)


def by_copies(layers, panels, covariance, data, drift):
    cols_here = covariance.shape[1]
    chips = SHARES // 2
    dma = pltpu.SemaphoreType.DMA
    scratch = [
        pltpu.VMEM((SHARES, K, SHARE, K * B), jnp.float32),
        pltpu.VMEM((SHARES, K, SHARE, cols_here + SIDES), jnp.float32),
        pltpu.VMEM((SHARES, K, SHARE, B), jnp.float32),
        pltpu.VMEM((SHARES, SHARE, cols_here + SIDES), jnp.float32),
    ]
    scratch += [pltpu.VMEM((2 * layers, high - low, SHARE, B), jnp.float32) for low, high in PARTS]
    scratch += [dma((SHARES,))] * 2 + [dma((layers, len(PARTS)))] * 2 + [dma((chips,))] * 4
    scratch += [dma((SHARES, len(PARTS)))] * 2 + [dma((chips, K))] * 4
    return call(
        copies_kernel, panels, covariance, data, drift, [], scratch, collective_id=0, has_side_effects=True
    )


def gather_by_sums(panels, row_tile, first_col, block):
    cols_here = block.shape[1] - SIDES
    col_tiles = cols_here // B
    mine = (panels == row_tile).astype(jnp.float32)
    rows = lax.psum((mine[:, None, None] * block[None]).reshape(K * B, -1), "row")
    parts = []
    for wanted in [panels[p] for p in range(K)] + [row_tile]:
        local = wanted - first_col
        held = (local >= 0) & (local < col_tiles)
        part = lax.dynamic_slice_in_dim(rows, jnp.clip(local, 0, col_tiles - 1) * B, B, 1)
        parts.append(jnp.where(held, part, 0.0))
    spread = lax.psum(jnp.concatenate(parts, axis=1), "col")
    return [
        part.reshape(K, SHARES, SHARE, -1).transpose(1, 0, 2, 3)
        for part in (spread[:, : K * B], rows, spread[:, K * B :])
    ]


def on_device(paired, layers, covariance, panels, observed, drift_basis):
    cols_here = covariance.shape[1]
    data = observed[None, :]
    if paired:
        complement, factor, data, drift = by_copies(layers, panels, covariance, data, drift_basis)
        return complement, factor, data[0], drift
    filler = jnp.zeros((SIDES - 1 - drift_basis.shape[0], B), jnp.float32)
    sides = jnp.concatenate([drift_basis, data, filler], axis=0)
    block = jnp.concatenate([covariance, sides.T], axis=1)
    first_col = lax.axis_index("col") * (cols_here // B)
    shares = gather_by_sums(panels, lax.axis_index("row"), first_col, block)
    complement, factor, data, drift = call(
        local_kernel, panels, covariance, data, drift_basis, shares, []
    )
    return complement, factor, data[0], drift


def solution(mesh):
    row, col = mesh.shape["row"], mesh.shape["col"]
    paired = row == SHARES and 2 * col == row
    return jax.shard_map(
        functools.partial(on_device, paired, col),
        mesh=mesh,
        in_specs=(P("row", "col"), P(), P("row"), P(None, "row")),
        out_specs=(P("row", "col"), P("row", None), P("row"), P(None, "row")),
        check_vma=False,
    )
```
